32 devices in a mesh: mom: 8 (over z, x), tm: 4 (over y, core).
Axes of the slice: x: 2, y: 2, z: 4, core: 2. Of those that a mesh axis runs over, the one named last changes fastest.
Arguments:
- green: bfloat16 [64, 32, 128, 1024], P('mom', None, None, 'tm'), may hold values from -6 to 6
- hole: bfloat16 [64, 32, 128, 1024], P('mom', None, None, 'tm'), may hold values from -6 to 6
- decay_log: float32 [64, 8, 1024], P('mom', None, 'tm'), as said below
- phase_step: float32 [64, 8, 1024], P('mom', None, 'tm'), may hold values from -1 to 1
Outputs:
- collision: bfloat16 [64, 32, 128, 1024], P('mom', None, None, 'tm')
The draws below stay inside these ranges and needn't reach their ends.
Inputs may be any that keep to these rules, and one draw needn't show every extreme that they name: decay_log holds logarithms of decay factors of at most one.
All inputs are finite; a program needn't handle non-finite values.
Results may differ from the reference program's by a relative error of at most 0.0067.
Values may be sent and summed in bfloat16 or wider, within the bound.
No kernel may reach another device: no remote copies, remote signals or barrier semaphores. Data moves between devices by JAX's collectives and lax.ppermute only.
A program may use at most 256 MiB of HBM per device.

```python
import math
import jax
import jax.numpy as jnp
from jax import lax

MOMENTA = 64
ORBITALS = 8
FIELD = 128
ROWS = 32
MEMORY_SLICES = 1024


def draw_decay_log(key, part):
    stochastic_seeds = jax.random.split(key, 6)
    chooser = jax.random.randint(stochastic_seeds[0], (MOMENTA, ORBITALS, 1), 0, 2)
    slow_mask = chooser == 1
    slow_rate = jnp.exp(jax.random.uniform(stochastic_seeds[1], (MOMENTA, ORBITALS, 1), jnp.float32, math.log(0.1 / MEMORY_SLICES), math.log(1.0 / MEMORY_SLICES)))
    fast_rate = jnp.exp(jax.random.uniform(stochastic_seeds[2], (MOMENTA, ORBITALS, 1), jnp.float32, math.log(1.0 / 50.0), math.log(1.0 / 30.0)))
    steady_damping = jnp.where(slow_mask, slow_rate, fast_rate)
    stochastic_jitter = jax.random.uniform(stochastic_seeds[3], (MOMENTA, ORBITALS, MEMORY_SLICES), jnp.float32, 0.5, 1.5)
    spike_location = jax.random.randint(stochastic_seeds[4], (3,), 0, MEMORY_SLICES)
    memory_lengths = jax.random.uniform(stochastic_seeds[5], (3,), jnp.float32, math.log(0.5), math.log(0.8))
    slice_ordinal = jnp.arange(MEMORY_SLICES, dtype=jnp.int32)
    spike_occurrences = jnp.sum(jnp.where(slice_ordinal[None, :] == spike_location[:, None], memory_lengths[:, None], 0.0), axis=0)
    return -steady_damping * stochastic_jitter + spike_occurrences[None, None, :]


def levels(rng, shape, cuts, smallest, largest):
    gain, own = 1.0, jax.random.fold_in(rng, 6)
    for dim, blocks in cuts:
        draws = jnp.exp(jax.random.uniform(jax.random.fold_in(own, dim), (blocks,), jnp.float32, smallest / len(cuts), largest / len(cuts)))
        gain = gain * jnp.repeat(draws, shape[dim] // blocks).reshape([-1 if axis == dim else 1 for axis in range(len(shape))])
    return gain


def normal_values(key, dims, scale, limit, cuts=(), kind=jnp.bfloat16):
    factor_of = levels(key, dims, cuts, -0.22, 0.18) if cuts else 1.0
    entries = jax.random.normal(key, dims, jnp.float32) * scale * factor_of
    return jnp.minimum(jnp.maximum(entries, -limit), limit).astype(kind)


def setup_inputs(seed: int = 0) -> dict:
    keys = jax.random.split(jax.random.key(seed), 5)
    return {
        "green": normal_values(keys[0], (MOMENTA, ROWS, FIELD, MEMORY_SLICES), 1.0, 6.0, ((0, 8), (3, 4))),
        "hole": normal_values(keys[1], (MOMENTA, ROWS, FIELD, MEMORY_SLICES), 1.0, 6.0, ((0, 8), (3, 4))),
        "decay_log": draw_decay_log(jax.random.fold_in(keys[4], 71), 0),
        "phase_step": jnp.clip(jax.random.uniform(keys[3], (MOMENTA, ORBITALS, MEMORY_SLICES), jnp.float32, -1.0, 1.0) * levels(keys[3], (MOMENTA, ORBITALS, MEMORY_SLICES), ((0, 8), (2, 4)), -0.4, 0.0), -1.0, 1.0),
    }


step_weight = 0.0625
coupling = 0.25

def transform_matrix(handed):
    numbers = jnp.arange(MOMENTA, dtype=jnp.int32)
    product = numbers[:, None] * numbers[None, :] % MOMENTA
    angles = product.astype(jnp.float32) * (2.0 * math.pi / MOMENTA)
    scaled = 1.0 / math.sqrt(MOMENTA)
    cosine = (jnp.cos(angles) * scaled).astype(jnp.bfloat16)
    sine = (handed * jnp.sin(angles) * scaled).astype(jnp.bfloat16)
    upper = jnp.stack([cosine, -sine], axis=-1)
    lower = jnp.stack([sine, cosine], axis=-1)
    return jnp.stack([upper, lower], axis=1)

def transform(matrix, field):
    return jnp.einsum('rokI,kpIC->rpoC', matrix.astype(jnp.float32), field.astype(jnp.float32), precision=lax.Precision.HIGHEST)

def self_energy(green_space, hole_space):
    green_re = green_space[:, :, 0, :]
    green_im = green_space[:, :, 1, :]
    hole_re = hole_space[:, :, 0, :]
    hole_im = hole_space[:, :, 1, :]
    square_re = green_re * green_re - green_im * green_im
    square_im = 2.0 * green_re * green_im
    energy_re = coupling * (square_re * hole_re - square_im * hole_im)
    energy_im = coupling * (square_re * hole_im + square_im * hole_re)
    return jnp.stack([energy_re, energy_im], axis=2).astype(jnp.bfloat16)

def reference(green, hole, decay_log, phase_step):
    plus = transform_matrix(1.0)
    minus = transform_matrix(-1.0)
    shrink = jnp.moveaxis(jnp.exp(decay_log), -1, 0)
    cosine = jnp.moveaxis(jnp.cos(phase_step), -1, 0)
    sine = jnp.moveaxis(jnp.sin(phase_step), -1, 0)
    pairs = ORBITALS * ORBITALS

    def one_row(row_index):
        green_row = lax.dynamic_index_in_dim(green, row_index, 1, keepdims=False)
        hole_row = lax.dynamic_index_in_dim(hole, row_index, 1, keepdims=False)
        green_split = green_row.reshape(MOMENTA, pairs, 2, MEMORY_SLICES)
        hole_split = hole_row.reshape(MOMENTA, pairs, 2, MEMORY_SLICES)
        green_space = transform(plus, green_split)
        hole_space = transform(minus, hole_split)
        sigma_space = self_energy(green_space, hole_space)
        sigma = transform(minus, sigma_space)
        sigma_cols = jnp.moveaxis(sigma.reshape(MOMENTA, ORBITALS, ORBITALS, 2, MEMORY_SLICES), -1, 0)

        def advance(carried, column):
            source, factor, turn_cos, turn_sin = column
            factor_wide = factor[:, None, :]
            cos_wide = turn_cos[:, None, :]
            sin_wide = turn_sin[:, None, :]
            new_re = factor_wide * (cos_wide * carried[..., 0] - sin_wide * carried[..., 1]) + source[..., 0]
            new_im = factor_wide * (sin_wide * carried[..., 0] + cos_wide * carried[..., 1]) + source[..., 1]
            updated = jnp.stack([new_re, new_im], axis=-1)
            return (updated, updated)
        start = jnp.zeros((MOMENTA, ORBITALS, ORBITALS, 2), jnp.float32)
        _, history = lax.scan(advance, start, (sigma_cols, shrink, cosine, sine))
        weighted = step_weight * history
        return jnp.moveaxis(weighted, 0, -1).reshape(MOMENTA, FIELD, MEMORY_SLICES).astype(jnp.bfloat16)
    rows_out = lax.map(one_row, jnp.arange(ROWS, dtype=jnp.int32))
    return jnp.moveaxis(rows_out, 0, 1)
```

```python
import functools
import math

import jax
import jax.numpy as jnp
from jax import lax
from jax.experimental import pallas as pl
from jax.experimental.pallas import tpu as pltpu
from jax.sharding import PartitionSpec as P

step_weight = 0.0625
coupling = 0.25
LANES = 128
VMEM = 56 * 1024 * 1024


def shift_columns(x, distance, fill):
    lane = lax.broadcasted_iota(jnp.int32, x.shape, 1)
    return jnp.where(lane >= distance, pltpu.roll(x, distance, 1), fill)


def product(a, b):
    return a[0] * b[0] - a[1] * b[1], a[0] * b[1] + a[1] * b[0]


def prepare_kernel(re_ref, im_ref, step_re, step_im, tile_re, tile_im, full_re, full_im):
    levels = step_re.shape[0]
    carry = None
    for tile in range(re_ref.shape[1] // LANES):
        cut = pl.ds(tile * LANES, LANES)
        base = (re_ref[:, cut], im_ref[:, cut])
        lane = lax.broadcasted_iota(jnp.int32, base[0].shape, 1)
        window = tuple(jnp.where(lane >= 1, part, 0.0) for part in base)
        running = base
        for level in range(levels):
            step_re[level, :, cut] = window[0]
            step_im[level, :, cut] = window[1]
            distance = 1 << level
            window = product(window, tuple(shift_columns(part, distance, 0.0) for part in window))
            running = product(
                running, tuple(shift_columns(part, distance, one) for part, one in zip(running, (1.0, 0.0)))
            )
        tile_re[:, cut] = running[0]
        tile_im[:, cut] = running[1]
        if carry is not None:
            running = product(running, tuple(jnp.broadcast_to(part, running[0].shape) for part in carry))
        full_re[:, cut] = running[0]
        full_im[:, cut] = running[1]
        carry = tuple(part[:, LANES - 1 : LANES] for part in running)


def prepare(lam_re, lam_im):
    rows, columns = lam_re.shape
    levels = int(math.log2(LANES))
    block = min(rows, 64)
    flat = pl.BlockSpec((block, columns), lambda i: (i, 0))
    deep = pl.BlockSpec((levels, block, columns), lambda i: (0, i, 0))
    one = jax.ShapeDtypeStruct((rows, columns), jnp.float32)
    many = jax.ShapeDtypeStruct((levels, rows, columns), jnp.float32)
    return pl.pallas_call(
        prepare_kernel,
        grid=(rows // block,),
        in_specs=[flat, flat],
        out_specs=[deep, deep, flat, flat, flat, flat],
        out_shape=[many, many, one, one, one, one],
        compiler_params=pltpu.CompilerParams(vmem_limit_bytes=VMEM),
        name="prepare",
    )(lam_re, lam_im)


def local_kernel(pieces, plus, minus, back, step_re, step_im, tile_re, tile_im, *refs):
    out_re, out_im, ends, energy, sigma = refs[-5:]
    depth, columns = energy.shape
    half = depth // 2
    levels = step_re.shape[0]
    index = pl.program_id(0) * pl.num_programs(1) + pl.program_id(1)

    def gather(which):
        return pieces[:, which].reshape(depth, columns)

    g = jnp.dot(plus[...], gather(0), preferred_element_type=jnp.float32)
    h = jnp.dot(minus[...], gather(1), preferred_element_type=jnp.float32)
    g_re, g_im, h_re, h_im = g[:half], g[half:], h[:half], h[half:]
    square_re = g_re * g_re - g_im * g_im
    square_im = 2.0 * g_re * g_im
    energy[:half] = (coupling * (square_re * h_re - square_im * h_im)).astype(jnp.bfloat16)
    energy[half:] = (coupling * (square_re * h_im + square_im * h_re)).astype(jnp.bfloat16)
    sigma[...] = jnp.dot(back[...], energy[...], preferred_element_type=jnp.float32)

    carry = None
    for tile in range(columns // LANES):
        cut = pl.ds(tile * LANES, LANES)
        state = (sigma[:half, cut], sigma[half:, cut])
        for level in range(levels):
            moved = tuple(pltpu.roll(part, 1 << level, 1) for part in state)
            added = product((step_re[level, :, cut], step_im[level, :, cut]), moved)
            state = (state[0] + added[0], state[1] + added[1])
        if carry is not None:
            wide = tuple(jnp.broadcast_to(part, state[0].shape) for part in carry)
            added = product((tile_re[:, cut], tile_im[:, cut]), wide)
            state = (state[0] + added[0], state[1] + added[1])
        out_re[0, :, cut] = state[0]
        out_im[0, :, cut] = state[1]
        carry = tuple(part[:, LANES - 1 : LANES] for part in state)
    lane = lax.broadcasted_iota(jnp.int32, (half, LANES), 1)
    for c in range(2):
        ends[c] = jnp.where(lane == index, jnp.broadcast_to(carry[c], (half, LANES)), ends[c])


def local_history(pieces, tables, steps, after):
    parts, _, kl, row_count, width, columns = pieces.shape
    depth = tables[0].shape[0]
    half = depth // 2
    field = depth // (kl * parts)
    grid = (row_count, width // field)
    piece = pl.BlockSpec((parts, 2, kl, 1, field, columns), lambda t, a: (0, 0, 0, t, a, 0))

    def whole(x):
        return pl.BlockSpec(x.shape, lambda t, a: (0,) * x.ndim, pipeline_mode=pl.Buffered(1))

    out = pl.BlockSpec((1, half, columns), lambda t, a: (t * grid[1] + a, 0, 0))
    number = grid[0] * grid[1]
    result = jax.ShapeDtypeStruct((number, half, columns), jnp.float32)
    constants = (*tables, *steps)
    return pl.pallas_call(
        local_kernel,
        grid=grid,
        in_specs=[piece]
        + [whole(x) for x in constants]
        + [pl.BlockSpec(memory_space=pl.ANY)] * len(after),
        out_specs=[out, out, pl.BlockSpec((2, half, LANES), lambda t, a: (0, 0, 0))],
        out_shape=[result, result, jax.ShapeDtypeStruct((2, half, LANES), jnp.float32)],
        scratch_shapes=[pltpu.VMEM((depth, columns), jnp.bfloat16), pltpu.VMEM((depth, columns), jnp.float32)],
        compiler_params=pltpu.CompilerParams(
            dimension_semantics=("arbitrary", "arbitrary"), vmem_limit_bytes=VMEM
        ),
        cost_estimate=pl.CostEstimate(
            flops=number * 30 * depth * depth * columns,
            bytes_accessed=number * depth * columns * 8,
            transcendentals=0,
        ),
        name="local_history",
    )(pieces, *constants, *after)


def finish_kernel(re_ref, im_ref, full_re, full_im, carry, weave, out):
    half, columns = full_re.shape
    index = pl.program_id(0) * pl.num_programs(1) + pl.program_id(1)
    group = weave.shape[0] // 2
    woven = []
    for i in range(half // group):
        rows = pl.ds(i * group, group)
        lane = lax.broadcasted_iota(jnp.int32, (group, LANES), 1)
        enter = tuple(
            jnp.sum(jnp.where(lane == index, carry[c, rows], 0.0), axis=1, keepdims=True) for c in range(2)
        )
        wide = tuple(jnp.broadcast_to(part, (group, columns)) for part in enter)
        added = product((full_re[rows], full_im[rows]), wide)
        both = jnp.concatenate(
            [
                (step_weight * (re_ref[0, rows] + added[0])).astype(jnp.bfloat16),
                (step_weight * (im_ref[0, rows] + added[1])).astype(jnp.bfloat16),
            ],
            axis=0,
        )
        woven.append(jnp.dot(weave[...], both, preferred_element_type=jnp.float32).astype(jnp.bfloat16))
    out[...] = jnp.concatenate(woven, axis=0).reshape(out.shape)


def finish(parts, momenta, local_re, local_im, full_re, full_im, carry, weave, grid):
    half, columns = full_re.shape
    field = 2 * half // momenta
    kl = momenta // parts
    step = pl.BlockSpec((1, half, columns), lambda t, a: (t * grid[1] + a, 0, 0))

    def whole(x):
        return pl.BlockSpec(x.shape, lambda t, a: (0,) * x.ndim, pipeline_mode=pl.Buffered(1))

    piece = pl.BlockSpec((parts, kl, 1, field, columns), lambda t, a: (0, 0, t, a, 0))
    return pl.pallas_call(
        finish_kernel,
        grid=grid,
        in_specs=[step, step, whole(full_re), whole(full_im), whole(carry), whole(weave)],
        out_specs=piece,
        out_shape=jax.ShapeDtypeStruct((parts, kl, grid[0], grid[1] * field, columns), jnp.bfloat16),
        compiler_params=pltpu.CompilerParams(
            dimension_semantics=("arbitrary", "arbitrary"), vmem_limit_bytes=VMEM
        ),
        cost_estimate=pl.CostEstimate(
            flops=grid[0] * grid[1] * half * columns * 10,
            bytes_accessed=grid[0] * grid[1] * half * columns * 30,
            transcendentals=0,
        ),
        name="finish",
    )(local_re, local_im, full_re, full_im, carry, weave)


def pack_kernel(green, hole, *refs):
    out = refs[-1]
    out[0, 0] = green[...]
    out[0, 1] = hole[...]


def pack(green, hole, parts, start, wide, after):
    kl, row_count, _, columns = green.shape
    share = row_count // parts
    steps = math.gcd(kl, 2)
    block = (kl // steps, share, wide, columns)
    inward = pl.BlockSpec(block, lambda j, i: (i, j, start // wide, 0))
    shape = (parts, 2, kl, share, wide, columns)
    return pl.pallas_call(
        pack_kernel,
        grid=(parts, steps),
        in_specs=[inward, inward] + [pl.BlockSpec(memory_space=pl.ANY)] * len(after),
        out_specs=pl.BlockSpec((1, 2, *block), lambda j, i: (j, 0, i, 0, 0, 0)),
        out_shape=jax.ShapeDtypeStruct(shape, green.dtype),
        compiler_params=pltpu.CompilerParams(vmem_limit_bytes=VMEM),
        cost_estimate=pl.CostEstimate(flops=0, bytes_accessed=4 * math.prod(shape), transcendentals=0),
        name="pack",
    )(green, hole, *after)


def place_kernel(pieces, *refs):
    refs[-1][...] = pieces[0]


def place(result, pieces, start, shape):
    parts, kl, share, wide, columns = pieces.shape
    held = [] if result is None else [result]
    steps = math.gcd(kl, 2)
    block = (kl // steps, share, wide, columns)
    return pl.pallas_call(
        place_kernel,
        grid=(parts, steps),
        in_specs=[pl.BlockSpec((1, *block), lambda j, i: (j, i, 0, 0, 0))]
        + [pl.BlockSpec(memory_space=pl.ANY)] * len(held),
        out_specs=pl.BlockSpec(block, lambda j, i: (i, j, start // wide, 0)),
        out_shape=jax.ShapeDtypeStruct(shape, pieces.dtype),
        input_output_aliases={1: 0} if held else {},
        compiler_params=pltpu.CompilerParams(vmem_limit_bytes=VMEM),
        cost_estimate=pl.CostEstimate(flops=0, bytes_accessed=4 * math.prod(pieces.shape), transcendentals=0),
        name="place",
    )(pieces, *held)


def entry(momenta, handed, site, out_part, momentum, in_part):
    angle = (site * momentum % momenta).astype(jnp.float32) * (2.0 * math.pi / momenta)
    scaled = 1.0 / math.sqrt(momenta)
    cosine = (jnp.cos(angle) * scaled).astype(jnp.bfloat16)
    sine = (handed * jnp.sin(angle) * scaled).astype(jnp.bfloat16)
    return jnp.where(out_part == in_part, cosine, jnp.where(out_part == 0, -sine, sine))


def transform_tables(momenta, orbitals, order):
    depth = momenta * orbitals * 2
    major = jnp.arange(depth, dtype=jnp.int32)
    field_k = jnp.repeat(order, orbitals * 2)
    field_b = major // 2 % orbitals
    field_c = major % 2
    inner_c = major // (momenta * orbitals)
    inner_r = major // orbitals % momenta
    inner_b = major % orbitals
    inner_k = jnp.tile(jnp.repeat(order, orbitals), 2)

    def table(handed, rows, cols):
        (r, b, o), (k, d, i) = (tuple(x[:, None] for x in rows), tuple(x[None, :] for x in cols))
        value = entry(momenta, handed, r, o, k, i)
        return jnp.where(b == d, value, jnp.zeros_like(value))

    inner = (inner_r, inner_b, inner_c)
    plus = table(1.0, inner, (field_k, field_b, field_c))
    minus = table(-1.0, inner, (field_k, field_b, field_c))
    back = table(-1.0, (inner_k, inner_b, inner_c), inner)
    return plus, minus, back


def weave_table(group):
    row = lax.broadcasted_iota(jnp.int32, (2 * group, 2 * group), 0)
    col = lax.broadcasted_iota(jnp.int32, (2 * group, 2 * group), 1)
    return (col == row // 2 + group * (row % 2)).astype(jnp.bfloat16)


def carries(axis, ends, total_re, total_im):
    devices, here = lax.axis_size(axis), lax.axis_index(axis)
    flat = jnp.swapaxes(ends, 1, 2)
    everything = lax.all_gather(flat, axis)
    state = (jnp.zeros_like(flat[0]), jnp.zeros_like(flat[1]))
    for k in range(devices - 1):
        moved = product((total_re[k][None, :], total_im[k][None, :]), state)
        new = (moved[0] + everything[k, 0], moved[1] + everything[k, 1])
        state = tuple(jnp.where(k < here, a, b) for a, b in zip(new, state))
    return jnp.swapaxes(jnp.stack(state), 1, 2)


def shards(green, hole, decay_log, phase_step):
    parts, here = lax.axis_size("mom"), lax.axis_index("mom")
    kl, row_count, width, columns = green.shape
    orbitals = decay_log.shape[1]
    momenta = kl * parts
    field = 2 * orbitals
    share = row_count // parts
    pairs = width // field
    sizes = [pairs // 2] * 2 if parts <= pairs else [pairs]
    starts = [sum(sizes[:i]) * field for i in range(len(sizes))]

    both = lax.all_gather(jnp.stack([decay_log, phase_step]), "mom", axis=1, tiled=True)
    damp, turn = (x.reshape(momenta * orbitals, columns) for x in both)
    decay = jnp.exp(damp)
    step_re, step_im, tile_re, tile_im, full_re, full_im = prepare(decay * jnp.cos(turn), decay * jnp.sin(turn))
    totals = lax.all_gather(jnp.stack([full_re[:, -1], full_im[:, -1]]), "tm")
    tables = transform_tables(momenta, orbitals, jnp.arange(momenta, dtype=jnp.int32))
    group = min(momenta, 8) * orbitals
    weave = weave_table(group)

    def exchange(x):
        return lax.all_to_all(x, "mom", split_axis=0, concat_axis=0, tiled=True)

    arrived = [
        exchange(pack(green, hole, parts, start, size * field, [both] if start == 0 else []))
        for start, size in zip(starts, sizes)
    ]
    result, after = None, []
    for pieces, start, size in zip(arrived, starts, sizes):
        local_re, local_im, ends = local_history(pieces, tables, (step_re, step_im, tile_re, tile_im), after)
        number = share * size
        enter = carries("tm", ends[:, :, :number], totals[:, 0], totals[:, 1])
        enter = jnp.pad(enter, ((0, 0), (0, 0), (0, LANES - number)))
        pieces = finish(parts, momenta, local_re, local_im, full_re, full_im, enter, weave, (share, size))
        after = [pieces]
        result = place(result, exchange(pieces), start, green.shape)
    return result


def solution(mesh):
    in_specs = (
        P("mom", None, None, "tm"),
        P("mom", None, None, "tm"),
        P("mom", None, "tm"),
        P("mom", None, "tm"),
    )
    out_specs = P("mom", None, None, "tm")
    return jax.shard_map(shards, mesh=mesh, in_specs=in_specs, out_specs=out_specs, check_vma=False)
```

```python
import functools
import math

import jax
import jax.numpy as jnp
from jax import lax
from jax.experimental import pallas as pl
from jax.experimental.pallas import tpu as pltpu
from jax.sharding import PartitionSpec as P

step_weight = 0.0625
coupling = 0.25
LANES = 128
VMEM = 56 * 1024 * 1024


def shift_columns(x, distance, fill):
    lane = lax.broadcasted_iota(jnp.int32, x.shape, 1)
    return jnp.where(lane >= distance, pltpu.roll(x, distance, 1), fill)


def product(a, b):
    return a[0] * b[0] - a[1] * b[1], a[0] * b[1] + a[1] * b[0]


def prepare_kernel(_, re_ref, im_ref, step_re, step_im, tile_re, tile_im, full_re, full_im):
    levels = step_re.shape[0]
    carry = None
    for tile in range(re_ref.shape[1] // LANES):
        cut = pl.ds(tile * LANES, LANES)
        base = (re_ref[:, cut], im_ref[:, cut])
        lane = lax.broadcasted_iota(jnp.int32, base[0].shape, 1)
        window = tuple(jnp.where(lane >= 1, part, 0.0) for part in base)
        running = base
        for level in range(levels):
            step_re[level, :, cut] = window[0]
            step_im[level, :, cut] = window[1]
            distance = 1 << level
            window = product(window, tuple(shift_columns(part, distance, 0.0) for part in window))
            running = product(
                running, tuple(shift_columns(part, distance, one) for part, one in zip(running, (1.0, 0.0)))
            )
        tile_re[:, cut] = running[0]
        tile_im[:, cut] = running[1]
        if carry is not None:
            running = product(running, tuple(jnp.broadcast_to(part, running[0].shape) for part in carry))
        full_re[:, cut] = running[0]
        full_im[:, cut] = running[1]
        carry = tuple(part[:, LANES - 1 : LANES] for part in running)


def prepare(positions, lam_re, lam_im):
    rows, columns = lam_re.shape
    levels = int(math.log2(LANES))
    block = rows // positions.shape[0]
    inward = pl.BlockSpec((block, columns), lambda i, positions: (positions[i], 0))
    flat = pl.BlockSpec((block, columns), lambda i, positions: (i, 0))
    deep = pl.BlockSpec((levels, block, columns), lambda i, positions: (0, i, 0))
    one = jax.ShapeDtypeStruct((rows, columns), jnp.float32)
    many = jax.ShapeDtypeStruct((levels, rows, columns), jnp.float32)
    return pl.pallas_call(
        prepare_kernel,
        grid_spec=pltpu.PrefetchScalarGridSpec(
            num_scalar_prefetch=1,
            grid=(rows // block,),
            in_specs=[inward, inward],
            out_specs=[deep, deep, flat, flat, flat, flat],
        ),
        out_shape=[many, many, one, one, one, one],
        compiler_params=pltpu.CompilerParams(vmem_limit_bytes=VMEM),
        name="prepare",
    )(positions, lam_re, lam_im)


def local_kernel(count, partner, *refs):
    pieces, constants, (out_re, out_im, ends, energy, sigma, field) = refs[:count], refs[count : count + 7], refs[-6:]
    plus, minus, back, step_re, step_im, tile_re, tile_im = constants
    depth, columns = energy.shape
    half = depth // 2
    levels = step_re.shape[0]
    index = pl.program_id(0) * pl.num_programs(1) + pl.program_id(1)

    if count == 1:
        field = pieces[0]
    else:
        for j, piece in enumerate(pieces):
            field[partner[j]] = piece[...]

    def gather(which):
        return field[:, which].reshape(depth, columns)

    g = jnp.dot(plus[...], gather(0), preferred_element_type=jnp.float32)
    h = jnp.dot(minus[...], gather(1), preferred_element_type=jnp.float32)
    g_re, g_im, h_re, h_im = g[:half], g[half:], h[:half], h[half:]
    square_re = g_re * g_re - g_im * g_im
    square_im = 2.0 * g_re * g_im
    energy[:half] = (coupling * (square_re * h_re - square_im * h_im)).astype(jnp.bfloat16)
    energy[half:] = (coupling * (square_re * h_im + square_im * h_re)).astype(jnp.bfloat16)
    sigma[...] = jnp.dot(back[...], energy[...], preferred_element_type=jnp.float32)

    carry = None
    for tile in range(columns // LANES):
        cut = pl.ds(tile * LANES, LANES)
        state = (sigma[:half, cut], sigma[half:, cut])
        for level in range(levels):
            moved = tuple(pltpu.roll(part, 1 << level, 1) for part in state)
            added = product((step_re[level, :, cut], step_im[level, :, cut]), moved)
            state = (state[0] + added[0], state[1] + added[1])
        if carry is not None:
            wide = tuple(jnp.broadcast_to(part, state[0].shape) for part in carry)
            added = product((tile_re[:, cut], tile_im[:, cut]), wide)
            state = (state[0] + added[0], state[1] + added[1])
        out_re[0, :, cut] = state[0]
        out_im[0, :, cut] = state[1]
        carry = tuple(part[:, LANES - 1 : LANES] for part in state)
    lane = lax.broadcasted_iota(jnp.int32, (half, LANES), 1)
    for c in range(2):
        ends[c] = jnp.where(lane == index, jnp.broadcast_to(carry[c], (half, LANES)), ends[c])


def local_history(pieces, partner, tables, steps, after):
    parts = partner.shape[0]
    kl, row_count, width, columns = pieces[0].shape[-4:]
    depth = tables[0].shape[0]
    half = depth // 2
    field = depth // (kl * parts)
    grid = (row_count, width // field)
    lead = pieces[0].ndim - 5
    block = (2, kl, 1, field, columns)
    piece = pl.BlockSpec((parts,) * lead + block, lambda t, a, p: (0,) * (lead + 2) + (t, a, 0))

    def whole(x):
        return pl.BlockSpec(x.shape, lambda t, a, p: (0,) * x.ndim, pipeline_mode=pl.Buffered(1))

    out = pl.BlockSpec((1, half, columns), lambda t, a, p: (t * grid[1] + a, 0, 0))
    number = grid[0] * grid[1]
    result = jax.ShapeDtypeStruct((number, half, columns), jnp.float32)
    constants = (*tables, *steps)
    return pl.pallas_call(
        functools.partial(local_kernel, len(pieces)),
        grid_spec=pltpu.PrefetchScalarGridSpec(
            num_scalar_prefetch=1,
            grid=grid,
            in_specs=[piece] * len(pieces)
            + [whole(x) for x in constants]
            + [pl.BlockSpec(memory_space=pl.ANY)] * len(after),
            out_specs=[out, out, pl.BlockSpec((2, half, LANES), lambda t, a, p: (0, 0, 0))],
            scratch_shapes=[
                pltpu.VMEM((depth, columns), jnp.bfloat16),
                pltpu.VMEM((depth, columns), jnp.float32),
                pltpu.VMEM((parts, *block), jnp.bfloat16),
            ],
        ),
        out_shape=[result, result, jax.ShapeDtypeStruct((2, half, LANES), jnp.float32)],
        compiler_params=pltpu.CompilerParams(
            dimension_semantics=("arbitrary", "arbitrary"), vmem_limit_bytes=VMEM
        ),
        cost_estimate=pl.CostEstimate(
            flops=number * 30 * depth * depth * columns,
            bytes_accessed=number * depth * columns * 8,
            transcendentals=0,
        ),
        name="local_history",
    )(partner, *pieces, *constants, *after)


def finish_kernel(count, partner, re_ref, im_ref, full_re, full_im, carry, weave, *refs):
    outs, hold = refs[-1 - count : -1], refs[-1]
    half, columns = full_re.shape
    index = pl.program_id(0) * pl.num_programs(1) + pl.program_id(1)
    group = weave.shape[0] // 2
    woven = []
    for i in range(half // group):
        rows = pl.ds(i * group, group)
        lane = lax.broadcasted_iota(jnp.int32, (group, LANES), 1)
        enter = tuple(
            jnp.sum(jnp.where(lane == index, carry[c, rows], 0.0), axis=1, keepdims=True) for c in range(2)
        )
        wide = tuple(jnp.broadcast_to(part, (group, columns)) for part in enter)
        added = product((full_re[rows], full_im[rows]), wide)
        both = jnp.concatenate(
            [
                (step_weight * (re_ref[0, rows] + added[0])).astype(jnp.bfloat16),
                (step_weight * (im_ref[0, rows] + added[1])).astype(jnp.bfloat16),
            ],
            axis=0,
        )
        woven.append(jnp.dot(weave[...], both, preferred_element_type=jnp.float32).astype(jnp.bfloat16))
    if count == 1:
        outs[0][...] = jnp.concatenate(woven, axis=0).reshape(outs[0].shape)
    else:
        hold[...] = jnp.concatenate(woven, axis=0).reshape(hold.shape)
        for j, out in enumerate(outs):
            out[...] = hold[partner[j]]


def finish(held, offset, total, partner, split, momenta, local_re, local_im, full_re, full_im, carry, weave, grid):
    parts = partner.shape[0]
    half, columns = full_re.shape
    field = 2 * half // momenta
    kl = momenta // parts
    step = pl.BlockSpec((1, half, columns), lambda t, a, p: (t * grid[1] + a, 0, 0))

    def whole(x):
        return pl.BlockSpec(x.shape, lambda t, a, p: (0,) * x.ndim, pipeline_mode=pl.Buffered(1))

    held = [] if held is None else [held]
    lead = () if split else (parts,)
    block = (kl, 1, field, columns)
    count = parts if split else 1
    return pl.pallas_call(
        functools.partial(finish_kernel, count),
        grid_spec=pltpu.PrefetchScalarGridSpec(
            num_scalar_prefetch=1,
            grid=grid,
            in_specs=[step, step, whole(full_re), whole(full_im), whole(carry), whole(weave)]
            + [pl.BlockSpec(memory_space=pl.ANY)] * len(held),
            out_specs=[pl.BlockSpec(lead + block, lambda t, a, p: (0,) * (len(lead) + 1) + (t, a + offset, 0))]
            * count,
            scratch_shapes=[pltpu.VMEM((parts, *block), jnp.bfloat16)],
        ),
        out_shape=[jax.ShapeDtypeStruct((*lead, kl, grid[0], total * field, columns), jnp.bfloat16)] * count,
        input_output_aliases={7: 0} if held else {},
        compiler_params=pltpu.CompilerParams(
            dimension_semantics=("arbitrary", "arbitrary"), vmem_limit_bytes=VMEM
        ),
        cost_estimate=pl.CostEstimate(
            flops=grid[0] * grid[1] * half * columns * 10,
            bytes_accessed=grid[0] * grid[1] * half * columns * 30,
            transcendentals=0,
        ),
        name="finish",
    )(partner, local_re, local_im, full_re, full_im, carry, weave, *held)


def pack_kernel(green, hole, *refs):
    out = refs[-1]
    out[0, 0] = green[...]
    out[0, 1] = hole[...]


def pack(held, green, hole, parts, some, start, wide, after):
    kl, row_count, _, columns = green.shape
    share = row_count // parts
    steps = math.gcd(kl, 2)
    block = (kl // steps, share, wide, columns)
    inward = pl.BlockSpec(block, lambda j, i: (i, j + some.start, start // wide, 0))
    shape = (parts, 2, kl, share, wide, columns)
    extra = ([] if held is None else [held]) + list(after)
    return pl.pallas_call(
        pack_kernel,
        grid=(len(some), steps),
        in_specs=[inward, inward] + [pl.BlockSpec(memory_space=pl.ANY)] * len(extra),
        out_specs=pl.BlockSpec((1, 2, *block), lambda j, i: (j + some.start, 0, i, 0, 0, 0)),
        out_shape=jax.ShapeDtypeStruct(shape, green.dtype),
        input_output_aliases={} if held is None else {2: 0},
        compiler_params=pltpu.CompilerParams(vmem_limit_bytes=VMEM),
        cost_estimate=pl.CostEstimate(
            flops=0, bytes_accessed=4 * math.prod(shape) * len(some) // parts, transcendentals=0
        ),
        name="pack",
    )(green, hole, *extra)


def place_kernel(pieces, *refs):
    refs[-1][...] = pieces[0]


def place(result, pieces, start, field, shape):
    parts, kl, share, wide, columns = pieces.shape
    held = [] if result is None else [result]
    held_wide = math.gcd(start, wide // field) * field
    block = (kl, share, held_wide, columns)
    return pl.pallas_call(
        place_kernel,
        grid=(parts, wide // held_wide),
        in_specs=[pl.BlockSpec((1, *block), lambda j, a: (j, 0, 0, a, 0))]
        + [pl.BlockSpec(memory_space=pl.ANY)] * len(held),
        out_specs=pl.BlockSpec(block, lambda j, a: (0, j, a + start * field // held_wide, 0)),
        out_shape=jax.ShapeDtypeStruct(shape, pieces.dtype),
        input_output_aliases={1: 0} if held else {},
        compiler_params=pltpu.CompilerParams(vmem_limit_bytes=VMEM),
        cost_estimate=pl.CostEstimate(flops=0, bytes_accessed=4 * math.prod(pieces.shape), transcendentals=0),
        name="place",
    )(pieces, *held)


def pack_one_kernel(_, green, hole, *refs):
    out = refs[-1]
    out[0] = green[...]
    out[1] = hole[...]


def pack_one(green, hole, row, parts, start, wide, after):
    kl, row_count, _, columns = green.shape
    share = row_count // parts
    shape = (2, kl, share, wide, columns)
    steps = math.gcd(kl, 4)
    block = (kl // steps, share, wide, columns)
    inward = pl.BlockSpec(block, lambda i, row: (i, row[0], start // wide, 0))
    return pl.pallas_call(
        pack_one_kernel,
        grid_spec=pltpu.PrefetchScalarGridSpec(
            num_scalar_prefetch=1,
            grid=(steps,),
            in_specs=[inward, inward] + [pl.BlockSpec(memory_space=pl.ANY)] * len(after),
            out_specs=pl.BlockSpec((2, *block), lambda i, row: (0, i, 0, 0, 0)),
        ),
        out_shape=jax.ShapeDtypeStruct(shape, green.dtype),
        compiler_params=pltpu.CompilerParams(vmem_limit_bytes=VMEM),
        cost_estimate=pl.CostEstimate(flops=0, bytes_accessed=4 * math.prod(shape), transcendentals=0),
        name="pack_one",
    )(row, green, hole, *after)


def place_list_kernel(count, rows, *refs):
    pieces, out = refs[:count], refs[-1]
    for i, piece in enumerate(pieces):

        @pl.when(pl.program_id(0) == i)
        def _():
            out[...] = piece[...]


def place_list(result, pieces, rows, start, shape):
    kl, share, wide, columns = pieces[0].shape
    held = [] if result is None else [result]
    count = len(pieces)
    steps = math.gcd(kl, 1)
    block = (kl // steps, share, wide, columns)

    def inward(which):
        return lambda i, k, rows: (jnp.where(i == which, k, jnp.where(i < which, 0, steps - 1)), 0, 0, 0)

    return pl.pallas_call(
        functools.partial(place_list_kernel, count),
        grid_spec=pltpu.PrefetchScalarGridSpec(
            num_scalar_prefetch=1,
            grid=(count, steps),
            in_specs=[pl.BlockSpec(block, inward(which)) for which in range(count)]
            + [pl.BlockSpec(memory_space=pl.ANY)] * len(held),
            out_specs=pl.BlockSpec(block, lambda i, k, rows: (k, rows[i], start // wide, 0)),
        ),
        out_shape=jax.ShapeDtypeStruct(shape, pieces[0].dtype),
        input_output_aliases={1 + count: 0} if held else {},
        compiler_params=pltpu.CompilerParams(vmem_limit_bytes=VMEM),
        cost_estimate=pl.CostEstimate(
            flops=0, bytes_accessed=4 * count * math.prod(pieces[0].shape), transcendentals=0
        ),
        name="place_list",
    )(rows, *pieces, *held)


def stack_kernel(a, b, *refs):
    refs[-1][0] = a[...]
    refs[-1][1] = b[...]


def stack_after(a, b, after):
    return pl.pallas_call(
        stack_kernel,
        in_specs=[pl.BlockSpec(memory_space=pltpu.VMEM)] * 2 + [pl.BlockSpec(memory_space=pl.ANY)] * len(after),
        out_shape=jax.ShapeDtypeStruct((2, *a.shape), a.dtype),
        name="stack_after",
    )(a, b, *after)


def entry(momenta, handed, site, out_part, momentum, in_part):
    angle = (site * momentum % momenta).astype(jnp.float32) * (2.0 * math.pi / momenta)
    scaled = 1.0 / math.sqrt(momenta)
    cosine = (jnp.cos(angle) * scaled).astype(jnp.bfloat16)
    sine = (handed * jnp.sin(angle) * scaled).astype(jnp.bfloat16)
    return jnp.where(out_part == in_part, cosine, jnp.where(out_part == 0, -sine, sine))


def transform_tables(momenta, orbitals, order):
    depth = momenta * orbitals * 2
    major = jnp.arange(depth, dtype=jnp.int32)
    field_k = jnp.repeat(order, orbitals * 2)
    field_b = major // 2 % orbitals
    field_c = major % 2
    inner_c = major // (momenta * orbitals)
    inner_r = major // orbitals % momenta
    inner_b = major % orbitals
    inner_k = jnp.tile(jnp.repeat(order, orbitals), 2)

    def table(handed, rows, cols):
        (r, b, o), (k, d, i) = (tuple(x[:, None] for x in rows), tuple(x[None, :] for x in cols))
        value = entry(momenta, handed, r, o, k, i)
        return jnp.where(b == d, value, jnp.zeros_like(value))

    inner = (inner_r, inner_b, inner_c)
    plus = table(1.0, inner, (field_k, field_b, field_c))
    minus = table(-1.0, inner, (field_k, field_b, field_c))
    back = table(-1.0, (inner_k, inner_b, inner_c), inner)
    return plus, minus, back


def weave_table(group):
    row = lax.broadcasted_iota(jnp.int32, (2 * group, 2 * group), 0)
    col = lax.broadcasted_iota(jnp.int32, (2 * group, 2 * group), 1)
    return (col == row // 2 + group * (row % 2)).astype(jnp.bfloat16)


def carries(axis, ends, total_re, total_im):
    devices, here = lax.axis_size(axis), lax.axis_index(axis)
    flat = jnp.swapaxes(ends, 1, 2)
    everything = lax.all_gather(flat, axis)
    state = (jnp.zeros_like(flat[0]), jnp.zeros_like(flat[1]))
    for k in range(devices - 1):
        moved = product((total_re[k][None, :], total_im[k][None, :]), state)
        new = (moved[0] + everything[k, 0], moved[1] + everything[k, 1])
        state = tuple(jnp.where(k < here, a, b) for a, b in zip(new, state))
    return jnp.swapaxes(jnp.stack(state), 1, 2)


def shards(green, hole, decay_log, phase_step):
    parts, here = lax.axis_size("mom"), lax.axis_index("mom")
    kl, row_count, width, columns = green.shape
    orbitals = decay_log.shape[1]
    momenta = kl * parts
    field = 2 * orbitals
    share = row_count // parts
    pairs = width // field
    middle = pairs // 2
    chunks = [(middle - 1, 1), (middle, middle), (0, middle - 1)] if parts <= pairs else [(0, pairs)]
    lone = len(chunks) > 1

    partners = [lax.bitwise_xor(here, jnp.int32(j)) for j in range(parts)]
    partner = jnp.stack(partners)

    def send(x, j):
        return x if j == 0 else lax.ppermute(x, "mom", [(i, i ^ j) for i in range(parts)])

    def exchange(x):
        return lax.all_to_all(x, "mom", split_axis=0, concat_axis=0, tiled=True)

    half = parts // 2
    far, near = list(range(half, parts))[::-1], list(range(1, half))
    mixed = [j for pair in zip(far, near + [None]) for j in pair if j]
    gathered = [j ^ bit for j in range(half) for bit in (0, half)]
    place_of = jnp.array([gathered.index(j) for j in range(parts)], jnp.int32)
    positions = place_of[partner]

    arrived, before, heard = [], [], []
    for index, (start, size) in enumerate(chunks):
        if lone and index == 0:
            pieces = [None] * parts
            for j in mixed + [0]:
                piece = pack_one(green, hole, partner[j][None], parts, start * field, size * field, [])
                pieces[j] = send(piece, j)
            before = pieces
        else:
            most, rest = range(parts - 1), range(parts - 1, parts)
            packed = pack(None, green, hole, parts, most, start * field, size * field, [])
            if not heard:
                after = [before[j] for j in far[:-1]] + [packed] if lone else []
                first = stack_after(decay_log, phase_step, after)
                both = jnp.concatenate([first, send(first, half)], axis=1)
            after = heard[1:] if heard else before + [both]
            packed = pack(packed, green, hole, parts, rest, start * field, size * field, after)
            pieces = [exchange(packed)]
            heard = heard or [send(both, j) for j in range(half)]
        arrived.append(pieces)

    both = jnp.concatenate(heard, axis=1)
    damp, turn = (x.reshape(momenta * orbitals, columns) for x in both)
    decay = jnp.exp(damp)
    step_re, step_im, tile_re, tile_im, full_re, full_im = prepare(
        positions, decay * jnp.cos(turn), decay * jnp.sin(turn)
    )
    totals = lax.all_gather(jnp.stack([full_re[:, -1], full_im[:, -1]]), "tm")
    tables = transform_tables(momenta, orbitals, jnp.arange(momenta, dtype=jnp.int32))
    group = min(momenta, 8) * orbitals
    weave = weave_table(group)

    result, finished, after = None, None, []
    for index, (pieces, (start, size)) in enumerate(zip(arrived, chunks)):
        local_re, local_im, ends = local_history(
            pieces, partner, tables, (step_re, step_im, tile_re, tile_im), after
        )
        number = share * size
        enter = carries("tm", ends[:, :, :number], totals[:, 0], totals[:, 1])
        enter = jnp.pad(enter, ((0, 0), (0, 0), (0, LANES - number)))
        joined = lone and index < 2
        first = chunks[0][0] if joined else start
        total = chunks[0][1] + chunks[1][1] if joined else size
        split = lone and index == 2
        outs = finish(
            finished if joined else None, start - first, total, partner, split, momenta,
            local_re, local_im, full_re, full_im, enter, weave, (share, size),
        )
        finished = outs[0]
        after = [finished]
        if split:
            order = [0] + near[1:] + far[:1] + near[:1] + far[1:]
            for some in order[:-3], order[-3:-1], order[-1:]:
                moved = [send(outs[j], j) for j in some]
                rows = jnp.stack([partner[j] for j in some])
                result = place_list(result, moved, rows, start * field, green.shape)
        elif not (lone and index == 0):
            result = place(result, exchange(finished), first, field, green.shape)
    return result


def solution(mesh):
    in_specs = (
        P("mom", None, None, "tm"),
        P("mom", None, None, "tm"),
        P("mom", None, "tm"),
        P("mom", None, "tm"),
    )
    out_specs = P("mom", None, None, "tm")
    return jax.shard_map(shards, mesh=mesh, in_specs=in_specs, out_specs=out_specs, check_vma=False)
```
